256 devices in a mesh: row: 8 (over y_hi, x), col: 32 (over y_lo, z, core).
Axes of the slice: x: 4, y: 4 (y_hi: 2, y_lo: 2; y = y_hi * 2 + y_lo), z: 8, core: 2. Of those that a mesh axis runs over, the one named last changes fastest.
Arguments:
- vectors: float32 [16384, 8192], P('row', 'col'), may hold values from -6 to 6
- panels: float32 [32, 16384, 256], P('col', 'row'), may hold values from -0.046875 to 0.046875
- factors: float32 [3, 256, 256], replicated, as said below
- owners: int32 [3], replicated, may hold values from 0 to 31
Outputs:
- updated: float32 [16384, 8192], P('row', 'col')
The draws below stay inside these ranges and needn't reach their ends.
Inputs may be any that keep to these rules, and one draw needn't show every extreme that they name: Each factors[k] is upper triangular with a positive diagonal. owners may repeat.
All inputs are finite; a program needn't handle non-finite values.
Results may differ from the reference program's by a relative error of at most 0.0002.
Values sent between devices are 32-bit elements; how exact they have to be, the bound alone decides.
A program may use at most 64 MiB of HBM per device.

```python
import jax
import jax.numpy as jnp
from jax import lax

WIDTH = 256
BLOCKS = 3
ROWS_TOTAL = 16384
VECTORS = 8192
N_COL = 32


def draw_factors(key, part):
    key = jax.random.fold_in(key, 11)
    key_diag, key_off = jax.random.split(key, 2)
    amplitude = (ROWS_TOTAL / WIDTH) ** 0.5
    diag_part = jax.random.uniform(key_diag, (BLOCKS, WIDTH), jnp.float32, 0.5, 2.0)
    off_part = 0.5 * jax.random.normal(key_off, (BLOCKS, WIDTH, WIDTH), jnp.float32)
    upper = jnp.triu(off_part, 1) / WIDTH ** 0.5
    eye_table = jnp.eye(WIDTH, dtype=jnp.float32)
    return (amplitude * (upper + eye_table[None, :, :] * diag_part[:, :, None])).astype(jnp.float32)


def level_of(key, dims, cuts, low, high):
    level = 1.0
    for position, blocks in cuts:
        steps = jax.random.uniform(jax.random.fold_in(jax.random.fold_in(key, 6), position), (blocks,), jnp.float32, low / len(cuts), high / len(cuts))
        level = level * jnp.repeat(jnp.exp(steps), dims[position] // blocks).reshape((-1,) + (1,) * (len(dims) - 1 - position))
    return level


def noise(stream_key, shape, deviation, most, pieces=(), held_as=jnp.bfloat16):
    entries = jax.random.normal(stream_key, shape, jnp.float32) * deviation
    if len(pieces) > 0:
        entries = level_of(stream_key, shape, pieces, -0.22, 0.18) * entries
    return jnp.clip(entries, min=-most, max=most).astype(held_as)


def setup_inputs(seed: int = 0) -> dict:
    splits = jax.random.split(jax.random.key(seed), 5)
    vectors = noise(splits[0], (ROWS_TOTAL, VECTORS), 1.0, 6.0, ((0, 8), (1, 32)), jnp.float32)
    panels = noise(splits[1], (N_COL, ROWS_TOTAL, WIDTH), ROWS_TOTAL ** -0.5, 0.046875, ((0, 32), (1, 8)), jnp.float32)
    factors = draw_factors(jax.random.fold_in(splits[4], 71), 0)
    owners = jax.random.randint(splits[3], (BLOCKS,), 0, N_COL).astype(jnp.int32)
    return dict(vectors=vectors, panels=panels, factors=factors, owners=owners)


def reference(vectors, panels, factors, owners):
    current = vectors
    for block in range(BLOCKS):
        reflector = panels[owners[block]]
        projected = jnp.dot(reflector.T, current, precision=lax.Precision.HIGHEST, preferred_element_type=jnp.float32)
        scaled = jnp.dot(factors[block], projected, precision=lax.Precision.HIGHEST, preferred_element_type=jnp.float32)
        current = current - jnp.dot(reflector, scaled, precision=lax.Precision.HIGHEST, preferred_element_type=jnp.float32)
    return current
```

```python
import functools

import jax
import jax.numpy as jnp
from jax import lax
from jax.experimental import pallas as pl
from jax.experimental.pallas import tpu as pltpu
from jax.sharding import PartitionSpec as P

MESH = pl.DeviceIdType.MESH
F32, BF16 = jnp.float32, jnp.bfloat16
BLOCKS = 3
WIDTH = 256
ROWS = 2048
PIECE = 64
CHUNK = 512
SHARE = 32
ORDER = (4, -3, 3, -2, 2, -1, 1, 0)
LONG, SHORT = 4, 3
WIDTHS = (256, 512, 768)
TN = (((0,), (0,)), ((), ()))


def halves(x):
    high = x.astype(BF16)
    return high, (x - high.astype(F32)).astype(BF16)


def dot3(a, b, dims=(((1,), (0,)), ((), ()))):
    def one(p, q):
        return lax.dot_general(p, q, dims, preferred_element_type=F32)

    return one(a[0], b[0]) + (one(a[0], b[1]) + one(a[1], b[0]))


def kernel(
    weights, c_ref, panel_ref, factors_ref, o_ref,
    c_v, c_hi, c_lo, f_v, v0, v1, v2, v_hi, v_lo,
    own, got, mine, passed, part0, part1, part2, sum0, sum1, sum2, in0, in1, in2, y_hi, y_lo,
    local_sem, first_s, first_r, rs_s, rs_r, ag_s, ag_r, core_s, core_r, row_s, row_r,
):
    v, part, total, arrived = (v0, v1, v2), (part0, part1, part2), (sum0, sum1, sum2), (in0, in1, in2)
    row, col = lax.axis_index("row"), lax.axis_index("col")
    yh, x = row // 4, row % 4
    yl, z, h = col // 16, (col // 2) % 8, col % 2
    sign = 1 - 2 * h

    def at(dyl, dz, dh):
        return (row, (yl ^ dyl) * 16 + lax.rem(z + 8 + dz, 8) * 2 + (h ^ dh))

    def rows_of(half, y, where):
        return pl.multiple_of(half * 1024 + lax.rem(z + 8 + where, 8) * 128 + y * PIECE, PIECE)

    def remote(src, dst, send, recv, device):
        return pltpu.make_async_remote_copy(
            src_ref=src, dst_ref=dst, send_sem=send, recv_sem=recv, device_id=device, device_id_type=MESH
        )

    sibling, partner, diagonal = at(0, 0, 1), at(1, 0, 0), at(1, 0, 1)
    ahead, behind = at(0, sign, 0), at(0, -sign, 0)
    peers = [((yh ^ (i // 4)) * 4 + (x + i % 4) % 4, col) for i in range(1, 8)]

    loads = [
        pltpu.make_async_copy(c_ref, c_v, local_sem.at[0]),
        pltpu.make_async_copy(factors_ref, f_v, local_sem.at[1]),
    ]
    for i, rel in enumerate(ORDER):
        loads.append(
            pltpu.make_async_copy(
                panel_ref.at[pl.ds(rows_of(h, yl, sign * rel), PIECE)], own.at[i], local_sem.at[2 + i]
            )
        )
    for load in loads:
        load.start()

    barrier = pltpu.get_barrier_semaphore()
    everyone = [sibling, partner, diagonal, ahead, behind] + peers
    for device in everyone:
        pl.semaphore_signal(barrier, inc=1, device_id=device, device_id_type=MESH)
    pl.semaphore_wait(barrier, len(everyone))

    sends = []

    def go(copy):
        copy.start()
        sends.append(copy)
        return copy

    first = []
    for i, rel in enumerate(ORDER):
        trio = []
        for s, (dy, dh, device) in enumerate(((1, 0, partner), (1, 1, diagonal), (0, 1, sibling))):
            way = sign * rel * (1 - 2 * dh)
            trio.append(
                go(
                    remote(
                        panel_ref.at[pl.ds(rows_of(h ^ dh, yl ^ dy, way), PIECE)],
                        got.at[s, i],
                        first_s.at[s, i],
                        first_r.at[s, i],
                        device,
                    )
                )
            )
        first.append(trio)

    loads[0].wait()

    @pl.loop(0, ROWS // CHUNK)
    def _(j):
        rows = pl.ds(pl.multiple_of(j * CHUNK, CHUNK), CHUNK)
        high, low = halves(c_v[rows, :])
        c_hi[rows, :] = high
        c_lo[rows, :] = low

    loads[1].wait()

    ready = set()

    def masked(k, i):
        if i not in ready:
            ready.add(i)
            loads[2 + i].wait()
            for copy in first[i]:
                copy.wait_recv()
        return (
            weights[k, 0] * own[i]
            + weights[k, 1] * got[0, i]
            + weights[k, 2] * got[1, i]
            + weights[k, 3] * got[2, i]
        )

    ring = {}
    for s in range(LONG):
        for k in range(BLOCKS):
            for way, hops, device in ((0, LONG, ahead), (1, SHORT, behind)):
                if s >= hops:
                    continue
                i = ORDER.index((hops - s) * (1 - 2 * way))
                value = masked(k, i)
                if s:
                    ring[k, way, s - 1].wait_recv()
                    value += passed[k, way, s - 1]
                mine[k, way, s] = value
                ring[k, way, s] = go(
                    remote(mine.at[k, way, s], passed.at[k, way, s], rs_s.at[k, way, s], rs_r.at[k, way, s], device)
                )

    spread, shared = {}, {}

    def share(k, y, where, slot):
        rows = pl.ds(rows_of(h, yl ^ y, where), PIECE)
        shared[k, y, slot] = go(
            remote(v[k].at[rows], v[k].at[rows], core_s.at[k, y, slot], core_r.at[k, y, slot], sibling)
        )

    def pass_on(k, y, way, s):
        direction = 1 - 2 * way
        rows = pl.ds(rows_of(h, yl ^ y, -sign * direction * s), PIECE)
        spread[k, y, way, s] = go(
            remote(
                v[k].at[rows], v[k].at[rows], ag_s.at[k, y, way, s], ag_r.at[k, y, way, s], ahead if way == 0 else behind
            )
        )

    beside = {}
    for k in range(BLOCKS):
        value = masked(k, 7)
        ring[k, 0, LONG - 1].wait_recv()
        ring[k, 1, SHORT - 1].wait_recv()
        rows = pl.ds(rows_of(h, yl, 0), PIECE)
        v[k][rows, :] = value + passed[k, 0, LONG - 1] + passed[k, 1, SHORT - 1]
        beside[k] = go(remote(v[k].at[rows], v[k].at[rows], ag_s.at[k, 0, 1, SHORT], ag_r.at[k, 0, 1, SHORT], partner))
        pass_on(k, 0, 0, 0)
        pass_on(k, 0, 1, 0)
        share(k, 0, 0, 7)
    for k in range(BLOCKS):
        beside[k].wait_recv()
        pass_on(k, 1, 0, 0)
        pass_on(k, 1, 1, 0)
        share(k, 1, 0, 7)

    def gather_step(k, s):
        for y in range(2):
            for way, hops in ((0, LONG), (1, SHORT)):
                if s >= hops:
                    continue
                spread[k, y, way, s].wait_recv()
                if s + 1 < hops:
                    pass_on(k, y, way, s + 1)
                direction = 1 - 2 * way
                share(k, y, -sign * direction * (s + 1), way * LONG + s)

    def products(k):
        for y in range(2):
            for slot in range(8):
                shared[k, y, slot].wait_recv()
        part[k][...] = jnp.zeros_like(part[k])

        @pl.loop(0, ROWS // CHUNK)
        def _(j):
            rows = pl.ds(pl.multiple_of(j * CHUNK, CHUNK), CHUNK)
            high, low = halves(v[k][rows, :])
            v_hi[k, rows, :] = high
            v_lo[k, rows, :] = low
            part[k][:, 0:WIDTH] += dot3((high, low), (c_hi[rows, :], c_lo[rows, :]), TN)
            for b in range(k):
                part[k][:, WIDTH * (b + 1) : WIDTH * (b + 2)] += dot3(
                    (high, low), (v_hi[b, rows, :], v_lo[b, rows, :]), TN
                )

    added, told = {}, {}

    def send_parts(k):
        for i, device in enumerate(peers):
            rows = pl.ds(pl.multiple_of(device[0] * SHARE, SHARE), SHARE)
            added[k, i] = go(remote(part[k].at[rows], arrived[k].at[i], row_s.at[k, 0, i], row_r.at[k, 0, i], device))

    def send_sums(k):
        rows = pl.ds(pl.multiple_of(row * SHARE, SHARE), SHARE)
        value = part[k][rows, :]
        for i in range(7):
            added[k, i].wait_recv()
            value += arrived[k][i]
        total[k][rows, :] = value
        for i, device in enumerate(peers):
            told[k, i] = go(remote(total[k].at[rows], total[k].at[rows], row_s.at[k, 1, i], row_r.at[k, 1, i], device))

    def solve(k):
        for i in range(7):
            told[k, i].wait_recv()
        value = total[k][:, 0:WIDTH]
        for b in range(k):
            value -= dot3(halves(total[k][:, WIDTH * (b + 1) : WIDTH * (b + 2)]), (y_hi[b], y_lo[b]))
        high, low = halves(dot3(halves(f_v[k]), halves(value)))
        y_hi[k] = high
        y_lo[k] = low

    def update(blocks):
        @pl.loop(0, ROWS // CHUNK)
        def _(j):
            rows = pl.ds(pl.multiple_of(j * CHUNK, CHUNK), CHUNK)
            value = c_v[rows, :]
            for k in blocks:
                value -= dot3((v_hi[k, rows, :], v_lo[k, rows, :]), (y_hi[k], y_lo[k]))
            c_v[rows, :] = value

    for t in range(LONG + BLOCKS - 1):
        for k in range(BLOCKS):
            if 0 <= t - k < LONG:
                gather_step(k, t - k)
        if t >= LONG - 1:
            k = t - LONG + 1
            products(k)
            send_parts(k)
            if k:
                send_sums(k - 1)
    solve(0)
    send_sums(BLOCKS - 1)
    solve(1)
    update((0, 1))
    solve(2)
    update((2,))
    store = pltpu.make_async_copy(c_v, o_ref, local_sem.at[0])
    store.start()
    for copy in sends:
        copy.wait_send()
    store.wait()


def shards(vectors, panels, factors, owners):
    col = lax.axis_index("col")
    held = jnp.stack([col, col ^ 16, col ^ 17, col ^ 1])
    weights = (owners[:, None] == held[None, :]).astype(F32)
    any_space = pl.BlockSpec(memory_space=pl.ANY)
    dma = pltpu.SemaphoreType.DMA
    tall = (ROWS, WIDTH)
    return pl.pallas_call(
        kernel,
        out_shape=jax.ShapeDtypeStruct(tall, F32),
        in_specs=[pl.BlockSpec(memory_space=pltpu.SMEM), any_space, any_space, any_space],
        out_specs=any_space,
        scratch_shapes=[
            pltpu.VMEM(tall, F32),
            pltpu.VMEM(tall, BF16),
            pltpu.VMEM(tall, BF16),
            pltpu.VMEM((BLOCKS, WIDTH, WIDTH), F32),
            *[pltpu.VMEM(tall, F32)] * BLOCKS,
            pltpu.VMEM((BLOCKS, *tall), BF16),
            pltpu.VMEM((BLOCKS, *tall), BF16),
            pltpu.VMEM((8, PIECE, WIDTH), F32),
            pltpu.VMEM((3, 8, PIECE, WIDTH), F32),
            pltpu.VMEM((BLOCKS, 2, LONG, PIECE, WIDTH), F32),
            pltpu.VMEM((BLOCKS, 2, LONG, PIECE, WIDTH), F32),
            *[pltpu.VMEM((WIDTH, w), F32) for w in WIDTHS],
            *[pltpu.VMEM((WIDTH, w), F32) for w in WIDTHS],
            *[pltpu.VMEM((7, SHARE, w), F32) for w in WIDTHS],
            pltpu.VMEM((BLOCKS, WIDTH, WIDTH), BF16),
            pltpu.VMEM((BLOCKS, WIDTH, WIDTH), BF16),
            dma((10,)),
            dma((3, 8)),
            dma((3, 8)),
            dma((BLOCKS, 2, LONG)),
            dma((BLOCKS, 2, LONG)),
            dma((BLOCKS, 2, 2, LONG)),
            dma((BLOCKS, 2, 2, LONG)),
            dma((BLOCKS, 2, 8)),
            dma((BLOCKS, 2, 8)),
            dma((BLOCKS, 2, 7)),
            dma((BLOCKS, 2, 7)),
        ],
        name="back_transform",
        compiler_params=pltpu.CompilerParams(
            collective_id=0, has_side_effects=True, vmem_limit_bytes=48 * 2**20
        ),
    )(weights, vectors, panels[0], factors)


def solution(mesh):
    placed = (P("row", "col"), P("col", "row", None), P(), P())
    return jax.shard_map(shards, mesh=mesh, in_specs=placed, out_specs=P("row", "col"), check_vma=False)
```

```python
import functools

import jax
import jax.numpy as jnp
from jax import lax
from jax.experimental import pallas as pl
from jax.experimental.pallas import tpu as pltpu
from jax.sharding import PartitionSpec as P

MESH = pl.DeviceIdType.MESH
F32, BF16 = jnp.float32, jnp.bfloat16
BLOCKS = 3
WIDTH = 256
HALF = WIDTH // 2
ROWS = 2048
GROUP = 256
CHUNK = 512
UNIT = 64
PIECES = (64, 32)
ORDER = (4, -3, 3, -2, 2, -1, 1, 0)
LONG, SHORT = 4, 3
HOPS = (LONG, SHORT)
SHARES = (32, 48, 64)
LAGS = (0, 0, 0)
NN = (((1,), (0,)), ((), ()))
NT = (((1,), (1,)), ((), ()))


def halves(x):
    high = x.astype(BF16)
    return high, (x - high.astype(F32)).astype(BF16)


def dot3(a, b, dims=NN):
    def one(p, q):
        return lax.dot_general(p, q, dims, preferred_element_type=F32)

    return one(a[0], b[0]) + (one(a[0], b[1]) + one(a[1], b[0]))


def kernel(
    owners, c_ref, panel_ref, factors_ref, o_ref,
    c_v, f_v, left_hi, left_lo, v0, v1, v2, v_hi, v_lo,
    own_a, own_b, got_a, got_b, mine_a, mine_b, passed_a, passed_b, half_a, other_a,
    part0, part1, part2, sum0, sum1, sum2, in0, in1, in2, gram1, gram2, yt_hi, yt_lo, y_hi, y_lo,
    local_sem, first_s, first_r, rs_s, rs_r, beside_s, beside_r, ag_s, ag_r, side_s, side_r, core_s, core_r, row_s, row_r,
    gram_s, gram_r,
):
    v, part, total, arrived = (v0, v1, v2), (part0, part1, part2), (sum0, sum1, sum2), (in0, in1, in2)
    gram = (None, gram1, gram2)
    mine, passed = (mine_a, mine_b), (passed_a, passed_b)
    row, col = lax.axis_index("row"), lax.axis_index("col")
    yh, x = row // 4, row % 4
    yl, z, h = col // 16, (col // 2) % 8, col % 2
    sign = 1 - 2 * h

    def along(where):
        return lax.rem(z + 8 + where, 8)

    def at(dyl, dz, dh):
        return (row, (yl ^ dyl) * 16 + along(dz) * 2 + (h ^ dh))

    def unit_rows(u, half, where):
        return pl.ds(pl.multiple_of(along(where) * GROUP + half * (GROUP // 2) + u * UNIT, UNIT), UNIT)

    def small_rows(half, y, where):
        start = along(where) * GROUP + half * (GROUP // 2) + UNIT + y * PIECES[1]
        return pl.ds(pl.multiple_of(start, PIECES[1]), PIECES[1])

    def group_rows(where):
        return pl.ds(pl.multiple_of(along(where) * GROUP, GROUP), GROUP)

    def remote(src, dst, send, recv, device):
        return pltpu.make_async_remote_copy(
            src_ref=src, dst_ref=dst, send_sem=send, recv_sem=recv, device_id=device, device_id_type=MESH
        )

    sibling, partner, diagonal = at(0, 0, 1), at(1, 0, 0), at(1, 0, 1)
    ahead, behind = at(0, sign, 0), at(0, -sign, 0)
    peers = [((yh ^ (i // 4)) * 4 + (x + i % 4) % 4, col) for i in range(1, 8)]

    barrier = pltpu.get_barrier_semaphore()
    everyone = [sibling, partner, diagonal, ahead, behind] + peers
    for device in everyone:
        pl.semaphore_signal(barrier, inc=1, device_id=device, device_id_type=MESH)

    load_c = pltpu.make_async_copy(c_ref, c_v, local_sem.at[0])
    load_f = pltpu.make_async_copy(factors_ref, f_v, local_sem.at[1])
    loads = []
    for i, rel in enumerate(ORDER):
        where = sign * rel
        loads.append(
            (
                pltpu.make_async_copy(panel_ref.at[unit_rows(0, h, where)], own_a.at[i], local_sem.at[2 + i]),
                pltpu.make_async_copy(panel_ref.at[small_rows(h, yl, where)], own_b.at[i], local_sem.at[10 + i]),
            )
        )
        for load in loads[-1]:
            load.start()
    load_c.start()
    load_f.start()

    held = (col, col ^ 16, col ^ 17, col ^ 1)
    weight = [[jnp.where(owners[k] == c, 1.0, 0.0).astype(F32) for c in held] for k in range(BLOCKS)]

    pl.semaphore_wait(barrier, len(everyone))

    sends = []

    def go(copy):
        copy.start()
        sends.append(copy)
        return copy

    first = [[None] * 4 for _ in ORDER]

    def bring(n):
        for i, rel in enumerate(ORDER):
            same, turned = sign * rel, -sign * rel
            src, dst, device = (
                (panel_ref.at[unit_rows(0, 1 - h, turned)], got_a.at[i], sibling),
                (panel_ref.at[small_rows(h, 1 - yl, same)], got_b.at[0, i], partner),
                (panel_ref.at[small_rows(1 - h, 1 - yl, turned)], got_b.at[1, i], diagonal),
                (panel_ref.at[small_rows(1 - h, yl, turned)], got_b.at[2, i], sibling),
            )[n]
            first[i][n] = go(remote(src, dst, first_s.at[n, i], first_r.at[n, i], device))

    for n in range(4):
        bring(n)

    ready = set()

    def masked(u, k, i):
        if (u, i) not in ready:
            ready.add((u, i))
            loads[i][u].wait()
            for copy in first[i][1:] if u else first[i][:1]:
                copy.wait_recv()
        w = weight[k]
        if u == 0:
            return w[0] * own_a[i] + w[3] * got_a[i]
        return w[0] * own_b[i] + w[1] * got_b[0, i] + w[2] * got_b[1, i] + w[3] * got_b[2, i]

    ring = {}

    def sum_step(u, k, s):
        for way, device in ((0, ahead), (1, behind)):
            if s >= HOPS[way]:
                continue
            value = masked(u, k, ORDER.index((HOPS[way] - s) * (1 - 2 * way)))
            if s:
                ring[u, k, way, s - 1].wait_recv()
                value += passed[u][k, way, s - 1]
            mine[u][k, way, s] = value
            ring[u, k, way, s] = go(
                remote(
                    mine[u].at[k, way, s],
                    passed[u].at[k, way, s],
                    rs_s.at[u, k, way, s],
                    rs_r.at[u, k, way, s],
                    device,
                )
            )

    def summed(u, k):
        value = masked(u, k, 7)
        for way in range(2):
            ring[u, k, way, HOPS[way] - 1].wait_recv()
            value += passed[u][k, way, HOPS[way] - 1]
        return value

    def left_of_c(begin, end):
        @pl.loop(begin, end)
        def _(j):
            rows = pl.ds(pl.multiple_of(j * CHUNK, CHUNK), CHUNK)
            high, low = halves(c_v[rows, :].T)
            left_hi[0:WIDTH, rows] = high
            left_lo[0:WIDTH, rows] = low

    beside, spread, side, shared = {}, {}, {}, {}

    def where_of(slot):
        return 0 if slot == 7 else sign * (slot - LONG + 1) if slot >= LONG else -sign * (slot + 1)

    def send_on(copies, key, rows, sems, device):
        k = key[0]
        copies[key] = go(remote(v[k].at[rows], v[k].at[rows], sems[0].at[key], sems[1].at[key], device))

    def share(k, kind, slot):
        where = where_of(slot)
        rows = unit_rows(0, h, where) if kind == 0 else small_rows(h, yl if kind == 1 else 1 - yl, where)
        send_on(shared, (k, kind, slot), rows, (core_s, core_r), sibling)

    def pass_on(k, u, way, s):
        where = -sign * (1 - 2 * way) * s
        rows = small_rows(h, yl, where) if u else unit_rows(0, h, where)
        send_on(spread, (k, u, way, s), rows, (ag_s, ag_r), behind if way else ahead)

    def cross(k, slot):
        send_on(side, (k, slot), small_rows(h, yl, where_of(slot)), (side_s, side_r), partner)

    def offer(k):
        half_a[k] = summed(0, k)
        beside[k] = go(remote(half_a.at[k], other_a.at[k], beside_s.at[k], beside_r.at[k], partner))

    def start(u, k):
        if u:
            v[k][small_rows(h, yl, 0), :] = summed(1, k)
        else:
            beside[k].wait_recv()
            v[k][unit_rows(0, h, 0), :] = half_a[k] + other_a[k]
        for way in range(2):
            pass_on(k, u, way, 0)
        if u:
            cross(k, 7)
        share(k, u, 7)

    def gather(u, k, s):
        for way in range(2):
            if s >= HOPS[way]:
                continue
            spread[k, u, way, s].wait_recv()
            if s + 1 < HOPS[way]:
                pass_on(k, u, way, s + 1)
            slot = way * LONG + s
            if u:
                cross(k, slot)
            share(k, u, slot)

    def slots_of(s):
        return (7,) if s < 0 else (s, LONG + s) if s < SHORT else (s,)

    def crossed(k, s):
        for slot in slots_of(s):
            side[k, slot].wait_recv()
            share(k, 2, slot)

    def products(k, s):
        for kind in range(3):
            for slot in slots_of(s):
                shared[k, kind, slot].wait_recv()
        for way in (1, -1) if 0 <= s < SHORT else (1,):
            rows = group_rows(way * (s + 1))
            value = v[k][rows, :]
            high, low = halves(value)
            v_hi[k, rows, :] = high
            v_lo[k, rows, :] = low
            tall = WIDTH + HALF * k
            if k + 1 < BLOCKS:
                mine_hi, mine_lo = halves(v[k][rows, pl.ds(pl.multiple_of(h * HALF, HALF), HALF)].T)
                left_hi[tall : tall + HALF, rows] = mine_hi
                left_lo[tall : tall + HALF, rows] = mine_lo
            out = dot3((left_hi[0:tall, rows], left_lo[0:tall, rows]), (high, low))
            pieces = [out[0:WIDTH].reshape(8, 32, WIDTH)]
            for b in range(k):
                pieces.append(out[WIDTH + HALF * b : WIDTH + HALF * (b + 1)].reshape(8, 16, WIDTH))
            start = 0
            for piece in pieces:
                stop = start + piece.shape[1]
                if s < 0:
                    part[k][:, start:stop, :] = piece
                else:
                    part[k][:, start:stop, :] += piece
                start = stop

    added, told, exchanged = {}, {}, {}

    def send_parts(k):
        for i, device in enumerate(peers):
            added[k, i] = go(
                remote(part[k].at[device[0]], arrived[k].at[i], row_s.at[k, 0, i], row_r.at[k, 0, i], device)
            )

    def send_sums(k):
        value = part[k][row]
        for i in range(7):
            added[k, i].wait_recv()
            value += arrived[k][i]
        total[k][row] = value
        for i, device in enumerate(peers):
            told[k, i] = go(remote(total[k].at[row], total[k].at[row], row_s.at[k, 1, i], row_r.at[k, 1, i], device))

    def swap_grams(k):
        for i in range(7):
            told[k, i].wait_recv()
        if k:
            src = total[k].at[:, pl.ds(32, 16 * k), :]
            exchanged[k] = go(remote(src, gram[k], gram_s.at[k], gram_r.at[k], sibling))

    def solve(k):
        value = total[k][:, 0:32, :].reshape(WIDTH, WIDTH)
        for b in range(k):
            mine_cols = pl.ds(pl.multiple_of(h * HALF, HALF), HALF)
            value -= dot3(
                (yt_hi[b, :, mine_cols], yt_lo[b, :, mine_cols]),
                halves(total[k][:, 32 + 16 * b : 48 + 16 * b, :].reshape(HALF, WIDTH)),
            )
        if k:
            exchanged[k].wait_recv()
        for b in range(k):
            other_cols = pl.ds(pl.multiple_of((1 - h) * HALF, HALF), HALF)
            value -= dot3(
                (yt_hi[b, :, other_cols], yt_lo[b, :, other_cols]),
                halves(gram[k][:, 16 * b : 16 * b + 16, :].reshape(HALF, WIDTH)),
            )
        value, factor = halves(value), halves(f_v[k])
        high, low = halves(dot3(factor, value, NT))
        y_hi[k] = high
        y_lo[k] = low
        if k + 1 < BLOCKS:
            high, low = halves(dot3(value, factor, NT))
            yt_hi[k] = high
            yt_lo[k] = low

    stores = []

    def update(blocks, last):
        for j in range(ROWS // CHUNK):
            rows = pl.ds(j * CHUNK, CHUNK)
            value = c_v[rows, :]
            for k in blocks:
                value -= dot3((v_hi[k, rows, :], v_lo[k, rows, :]), (y_hi[k], y_lo[k]))
            c_v[rows, :] = value
            if last:
                stores.append(pltpu.make_async_copy(c_v.at[rows], o_ref.at[rows], local_sem.at[2 + j]))
                stores[-1].start()

    def each(step, *args):
        for k in range(BLOCKS):
            step(*args[:1], k, *args[1:])

    A, B = functools.partial(sum_step, 0), functools.partial(sum_step, 1)
    gather_a, gather_b = functools.partial(gather, 0), functools.partial(gather, 1)
    turns = (
        ((A, 0),),
        ((A, 1),),
        ((A, 2),),
        ((A, 3), (B, 0)),
        ((offer,), (B, 1)),
        ((functools.partial(start, 0),), (B, 2)),
        ((gather_a, 0), (B, 3)),
        ((gather_a, 1), (functools.partial(start, 1),)),
        ((gather_a, 2), (gather_b, 0)),
        ((gather_a, 3), (gather_b, 1), (crossed, -1)),
        ((gather_b, 2), (crossed, 0), (products, -1)),
        ((gather_b, 3), (crossed, 1), (products, 0)),
        ((crossed, 2), (products, 1)),
        ((crossed, 3), (products, 2)),
        ((products, 3), (send_parts,)),
        (),
        ((send_sums,),),
    )
    load_c.wait()
    load_f.wait()
    for t in range(len(turns) + max(LAGS)):
        for k in range(BLOCKS):
            if 0 <= t - LAGS[k] < len(turns):
                for step, *args in turns[t - LAGS[k]]:
                    step(k, *args)
            if t == 0 and k < 2:
                left_of_c(2 * k, 2 * k + 2)
    swap_grams(0)
    solve(0)
    swap_grams(1)
    solve(1)
    update((0, 1), False)
    swap_grams(2)
    solve(2)
    update((2,), True)
    for copy in sends:
        copy.wait_send()
    for store in stores:
        store.wait()


def shards(vectors, panels, factors, owners):
    any_space = pl.BlockSpec(memory_space=pl.ANY)
    dma = pltpu.SemaphoreType.DMA
    tall = (ROWS, WIDTH)
    square = (WIDTH, WIDTH)
    return pl.pallas_call(
        kernel,
        out_shape=jax.ShapeDtypeStruct(tall, F32),
        in_specs=[pl.BlockSpec(memory_space=pltpu.SMEM), any_space, any_space, any_space],
        out_specs=any_space,
        scratch_shapes=[
            pltpu.VMEM(tall, F32),
            pltpu.VMEM((BLOCKS, *square), F32),
            pltpu.VMEM((2 * WIDTH, ROWS), BF16),
            pltpu.VMEM((2 * WIDTH, ROWS), BF16),
            *[pltpu.VMEM(tall, F32)] * BLOCKS,
            pltpu.VMEM((BLOCKS, *tall), BF16),
            pltpu.VMEM((BLOCKS, *tall), BF16),
            *[pltpu.VMEM((8, p, WIDTH), F32) for p in PIECES],
            pltpu.VMEM((8, PIECES[0], WIDTH), F32),
            pltpu.VMEM((3, 8, PIECES[1], WIDTH), F32),
            *[pltpu.VMEM((BLOCKS, 2, LONG, p, WIDTH), F32) for p in PIECES],
            *[pltpu.VMEM((BLOCKS, 2, LONG, p, WIDTH), F32) for p in PIECES],
            pltpu.VMEM((BLOCKS, UNIT, WIDTH), F32),
            pltpu.VMEM((BLOCKS, UNIT, WIDTH), F32),
            *[pltpu.VMEM((8, n, WIDTH), F32) for n in SHARES],
            *[pltpu.VMEM((8, n, WIDTH), F32) for n in SHARES],
            *[pltpu.VMEM((7, n, WIDTH), F32) for n in SHARES],
            pltpu.VMEM((8, 16, WIDTH), F32),
            pltpu.VMEM((8, 32, WIDTH), F32),
            *[pltpu.VMEM((BLOCKS, *square), BF16)] * 4,
            dma((18,)),
            dma((4, 8)),
            dma((4, 8)),
            dma((2, BLOCKS, 2, LONG)),
            dma((2, BLOCKS, 2, LONG)),
            dma((BLOCKS,)),
            dma((BLOCKS,)),
            dma((BLOCKS, 2, 2, LONG)),
            dma((BLOCKS, 2, 2, LONG)),
            dma((BLOCKS, 8)),
            dma((BLOCKS, 8)),
            dma((BLOCKS, 3, 8)),
            dma((BLOCKS, 3, 8)),
            dma((BLOCKS, 2, 7)),
            dma((BLOCKS, 2, 7)),
            dma((BLOCKS,)),
            dma((BLOCKS,)),
        ],
        name="back_transform",
        compiler_params=pltpu.CompilerParams(
            collective_id=0, has_side_effects=True, vmem_limit_bytes=60 * 2**20
        ),
    )(owners, vectors, panels[0], factors)


def solution(mesh):
    placed = (P("row", "col"), P("col", "row", None), P(), P())
    return jax.shard_map(shards, mesh=mesh, in_specs=placed, out_specs=P("row", "col"), check_vma=False)
```

```python
import functools

import jax
import jax.numpy as jnp
from jax import lax
from jax.experimental import pallas as pl
from jax.experimental.pallas import tpu as pltpu
from jax.sharding import PartitionSpec as P

MESH = pl.DeviceIdType.MESH
F32, BF16 = jnp.float32, jnp.bfloat16
BLOCKS = 3
WIDTH = 256
HALF = WIDTH // 2
ROWS = 2048
GROUP = 256
CHUNK = 512
UNIT = 64
PIECES = (64, 32)
ORDER = (4, -3, 3, -2, 2, -1, 1, 0)
LONG, SHORT = 4, 3
HOPS = (LONG, SHORT)
SHARE = 32
STRIP = 16
PAIRS = ((0, 1), (0, 2), (1, 2))
TILE = 8
LAGS = (0, 0, 0)
NN = (((1,), (0,)), ((), ()))
NT = (((1,), (1,)), ((), ()))


def halves(x):
    high = x.astype(BF16)
    return high, (x - high.astype(F32)).astype(BF16)


def dot3(a, b, dims=NN):
    def one(p, q):
        return lax.dot_general(p, q, dims, preferred_element_type=F32)

    return one(a[0], b[0]) + (one(a[0], b[1]) + one(a[1], b[0]))


def kernel(
    owners, c_ref, panel_ref, factors_ref, o_ref,
    c_v, f_v, left_hi, left_lo, v0, v1, v2, v_hi, v_lo,
    own_a, own_b, got_a, got_b, mine_a, mine_b, passed_a, passed_b, half_a, other_a,
    part, total, arrived, turned, strip, strip_in, strip_sum, gram, yt_hi, yt_lo, y_hi, y_lo,
    local_sem, first_s, first_r, rs_s, rs_r, beside_s, beside_r, ag_s, ag_r, side_s, side_r, core_s, core_r, row_s, row_r,
    strip_s, strip_r, plane_s, plane_r, gram_s, gram_r,
):
    v = (v0, v1, v2)
    mine, passed = (mine_a, mine_b), (passed_a, passed_b)
    row, col = lax.axis_index("row"), lax.axis_index("col")
    yh, x = row // 4, row % 4
    yl, z, h = col // 16, (col // 2) % 8, col % 2
    sign = 1 - 2 * h

    def along(where):
        return lax.rem(z + 8 + where, 8)

    def at(dyl, dz, dh):
        return (row, (yl ^ dyl) * 16 + along(dz) * 2 + (h ^ dh))

    def unit_rows(u, half, where):
        return pl.ds(pl.multiple_of(along(where) * GROUP + half * (GROUP // 2) + u * UNIT, UNIT), UNIT)

    def small_rows(half, y, where):
        start = along(where) * GROUP + half * (GROUP // 2) + UNIT + y * PIECES[1]
        return pl.ds(pl.multiple_of(start, PIECES[1]), PIECES[1])

    def group_rows(where):
        return pl.ds(pl.multiple_of(along(where) * GROUP, GROUP), GROUP)

    def remote(src, dst, send, recv, device):
        return pltpu.make_async_remote_copy(
            src_ref=src, dst_ref=dst, send_sem=send, recv_sem=recv, device_id=device, device_id_type=MESH
        )

    sibling, partner, diagonal = at(0, 0, 1), at(1, 0, 0), at(1, 0, 1)
    ahead, behind = at(0, sign, 0), at(0, -sign, 0)
    peers = [((yh ^ (i // 4)) * 4 + (x + i % 4) % 4, col) for i in range(1, 8)]

    barrier = pltpu.get_barrier_semaphore()
    mates = [at(0, i, 0) for i in range(1, 8)]
    everyone = [sibling, partner, diagonal] + mates + peers
    for device in everyone:
        pl.semaphore_signal(barrier, inc=1, device_id=device, device_id_type=MESH)

    load_c = pltpu.make_async_copy(c_ref, c_v, local_sem.at[0])
    load_f = pltpu.make_async_copy(factors_ref, f_v, local_sem.at[1])
    loads = []
    for i, rel in enumerate(ORDER):
        where = sign * rel
        loads.append(
            (
                pltpu.make_async_copy(panel_ref.at[unit_rows(0, h, where)], own_a.at[i], local_sem.at[2 + i]),
                pltpu.make_async_copy(panel_ref.at[small_rows(h, yl, where)], own_b.at[i], local_sem.at[10 + i]),
            )
        )
        for load in loads[-1]:
            load.start()
    load_c.start()
    load_f.start()

    held = (col, col ^ 16, col ^ 17, col ^ 1)
    weight = [[jnp.where(owners[k] == c, 1.0, 0.0).astype(F32) for c in held] for k in range(BLOCKS)]

    pl.semaphore_wait(barrier, len(everyone))

    sends = []

    def go(copy):
        copy.start()
        sends.append(copy)
        return copy

    first = [[None] * 4 for _ in ORDER]

    def bring(n):
        for i, rel in enumerate(ORDER):
            same, turned = sign * rel, -sign * rel
            src, dst, device = (
                (panel_ref.at[unit_rows(0, 1 - h, turned)], got_a.at[i], sibling),
                (panel_ref.at[small_rows(h, 1 - yl, same)], got_b.at[0, i], partner),
                (panel_ref.at[small_rows(1 - h, 1 - yl, turned)], got_b.at[1, i], diagonal),
                (panel_ref.at[small_rows(1 - h, yl, turned)], got_b.at[2, i], sibling),
            )[n]
            first[i][n] = go(remote(src, dst, first_s.at[n, i], first_r.at[n, i], device))

    for n in range(4):
        bring(n)

    ready = set()

    def masked(u, k, i):
        if (u, i) not in ready:
            ready.add((u, i))
            loads[i][u].wait()
            for copy in first[i][1:] if u else first[i][:1]:
                copy.wait_recv()
        w = weight[k]
        if u == 0:
            return w[0] * own_a[i] + w[3] * got_a[i]
        return w[0] * own_b[i] + w[1] * got_b[0, i] + w[2] * got_b[1, i] + w[3] * got_b[2, i]

    ring = {}

    def sum_step(u, k, s):
        for way, device in ((0, ahead), (1, behind)):
            if s >= HOPS[way]:
                continue
            value = masked(u, k, ORDER.index((HOPS[way] - s) * (1 - 2 * way)))
            if s:
                ring[u, k, way, s - 1].wait_recv()
                value += passed[u][k, way, s - 1]
            mine[u][k, way, s] = value
            ring[u, k, way, s] = go(
                remote(
                    mine[u].at[k, way, s],
                    passed[u].at[k, way, s],
                    rs_s.at[u, k, way, s],
                    rs_r.at[u, k, way, s],
                    device,
                )
            )

    def summed(u, k):
        value = masked(u, k, 7)
        for way in range(2):
            ring[u, k, way, HOPS[way] - 1].wait_recv()
            value += passed[u][k, way, HOPS[way] - 1]
        return value

    def left_of_c(begin, end):
        @pl.loop(begin, end)
        def _(j):
            rows = pl.ds(pl.multiple_of(j * CHUNK, CHUNK), CHUNK)
            high, low = halves(c_v[rows, :].T)
            left_hi[0:WIDTH, rows] = high
            left_lo[0:WIDTH, rows] = low

    beside, spread, side, shared = {}, {}, {}, {}

    def where_of(slot):
        return 0 if slot == 7 else sign * (slot - LONG + 1) if slot >= LONG else -sign * (slot + 1)

    def send_on(copies, key, rows, sems, device):
        k = key[0]
        copies[key] = go(remote(v[k].at[rows], v[k].at[rows], sems[0].at[key], sems[1].at[key], device))

    def share(k, kind, slot):
        where = where_of(slot)
        rows = unit_rows(0, h, where) if kind == 0 else small_rows(h, yl if kind == 1 else 1 - yl, where)
        send_on(shared, (k, kind, slot), rows, (core_s, core_r), sibling)

    def pass_on(k, u, way, s):
        where = -sign * (1 - 2 * way) * s
        rows = small_rows(h, yl, where) if u else unit_rows(0, h, where)
        send_on(spread, (k, u, way, s), rows, (ag_s, ag_r), behind if way else ahead)

    def cross(k, slot):
        send_on(side, (k, slot), small_rows(h, yl, where_of(slot)), (side_s, side_r), partner)

    def offer(k):
        half_a[k] = summed(0, k)
        beside[k] = go(remote(half_a.at[k], other_a.at[k], beside_s.at[k], beside_r.at[k], partner))

    def start(u, k):
        if u:
            v[k][small_rows(h, yl, 0), :] = summed(1, k)
        else:
            beside[k].wait_recv()
            v[k][unit_rows(0, h, 0), :] = half_a[k] + other_a[k]
        for way in range(2):
            pass_on(k, u, way, 0)
        if u:
            cross(k, 7)
        share(k, u, 7)

    def gather(u, k, s):
        for way in range(2):
            if s >= HOPS[way]:
                continue
            spread[k, u, way, s].wait_recv()
            if s + 1 < HOPS[way]:
                pass_on(k, u, way, s + 1)
            slot = way * LONG + s
            if u:
                cross(k, slot)
            share(k, u, slot)

    def slots_of(s):
        return (7,) if s < 0 else (s, LONG + s) if s < SHORT else (s,)

    def crossed(k, s):
        for slot in slots_of(s):
            side[k, slot].wait_recv()
            share(k, 2, slot)

    def products(k, s):
        for kind in range(3):
            for slot in slots_of(s):
                shared[k, kind, slot].wait_recv()
        for way in (1, -1) if 0 <= s < SHORT else (1,):
            rows = group_rows(way * (s + 1))
            value = v[k][rows, :]
            high, low = halves(value)
            v_hi[k, rows, :] = high
            v_lo[k, rows, :] = low
            tall = WIDTH + STRIP * k
            if k + 1 < BLOCKS:
                turned[...] = v[k][rows, pl.ds(pl.multiple_of(h * HALF, HALF), HALF)].T
                mine_hi, mine_lo = halves(turned[pl.ds(pl.multiple_of(z * STRIP, STRIP), STRIP), :])
                left_hi[tall : tall + STRIP, rows] = mine_hi
                left_lo[tall : tall + STRIP, rows] = mine_lo
            out = dot3((left_hi[0:tall, rows], left_lo[0:tall, rows]), (high, low))
            pieces = [(part.at[k], out[0:WIDTH].reshape(8, SHARE, WIDTH))]
            for b in range(k):
                n = PAIRS.index((b, k))
                begin = WIDTH + STRIP * b
                pieces.append((strip.at[2 * n : 2 * n + 2], out[begin : begin + STRIP].reshape(2, TILE, WIDTH)))
            for ref, piece in pieces:
                if s < 0:
                    ref[...] = piece
                else:
                    ref[...] += piece

    added, told, strips, planes = {}, {}, {}, {}

    def send_parts(k):
        for i, device in enumerate(peers):
            added[k, i] = go(
                remote(part.at[k, device[0]], arrived.at[k, i], row_s.at[k, 0, i], row_r.at[k, 0, i], device)
            )

    def send_sums(k):
        value = part[k, row]
        for i in range(7):
            added[k, i].wait_recv()
            value += arrived[k, i]
        total[k, row] = value
        for i, device in enumerate(peers):
            told[k, i] = go(remote(total.at[k, row], total.at[k, row], row_s.at[k, 1, i], row_r.at[k, 1, i], device))

    def send_strips():
        strip[6:8] = jnp.zeros((2, TILE, WIDTH), F32)
        for i, device in enumerate(peers):
            strips[0, i] = go(remote(strip.at[device[0]], strip_in.at[i], strip_s.at[0, i], strip_r.at[0, i], device))

    def send_strip_sums():
        value = strip[row]
        for i in range(7):
            strips[0, i].wait_recv()
            value += strip_in[i]
        strip_sum[row] = value
        for i, device in enumerate(peers):
            strips[1, i] = go(
                remote(strip_sum.at[row], strip_sum.at[row], strip_s.at[1, i], strip_r.at[1, i], device)
            )

    def spread_grams():
        for i in range(7):
            strips[1, i].wait_recv()
        gram[h, z] = strip_sum[0:6]
        for i, device in enumerate(mates):
            planes[i] = go(remote(gram.at[h, z], gram.at[h, z], plane_s.at[i], plane_r.at[i], device))

    def swap_grams():
        for i in range(7):
            planes[i].wait_recv()
        planes[7] = go(remote(gram.at[h], gram.at[h], gram_s, gram_r, sibling))

    def solve(k):
        for i in range(7):
            told[k, i].wait_recv()
        value = total[k].reshape(WIDTH, WIDTH)
        for b in range(k):
            n = PAIRS.index((b, k))
            for half in range(2):
                value -= dot3(
                    (yt_hi[b, :, half * HALF : (half + 1) * HALF], yt_lo[b, :, half * HALF : (half + 1) * HALF]),
                    halves(gram[half, :, 2 * n : 2 * n + 2].reshape(HALF, WIDTH)),
                )
        value, factor = halves(value), halves(f_v[k])
        high, low = halves(dot3(factor, value, NT))
        y_hi[k] = high
        y_lo[k] = low
        if k + 1 < BLOCKS:
            high, low = halves(dot3(value, factor, NT))
            yt_hi[k] = high
            yt_lo[k] = low

    stores = []

    def update(blocks, last):
        for j in range(ROWS // CHUNK):
            rows = pl.ds(j * CHUNK, CHUNK)
            value = c_v[rows, :]
            for k in blocks:
                value -= dot3((v_hi[k, rows, :], v_lo[k, rows, :]), (y_hi[k], y_lo[k]))
            c_v[rows, :] = value
            if last:
                stores.append(pltpu.make_async_copy(c_v.at[rows], o_ref.at[rows], local_sem.at[2 + j]))
                stores[-1].start()

    def each(step, *args):
        for k in range(BLOCKS):
            step(*args[:1], k, *args[1:])

    A, B = functools.partial(sum_step, 0), functools.partial(sum_step, 1)
    gather_a, gather_b = functools.partial(gather, 0), functools.partial(gather, 1)
    turns = (
        ((A, 0),),
        ((A, 1),),
        ((A, 2),),
        ((A, 3), (B, 0)),
        ((offer,), (B, 1)),
        ((functools.partial(start, 0),), (B, 2)),
        ((gather_a, 0), (B, 3)),
        ((gather_a, 1), (functools.partial(start, 1),)),
        ((gather_a, 2), (gather_b, 0)),
        ((gather_a, 3), (gather_b, 1), (crossed, -1)),
        ((gather_b, 2), (crossed, 0), (products, -1)),
        ((gather_b, 3), (crossed, 1), (products, 0)),
        ((crossed, 2), (products, 1)),
        ((crossed, 3), (products, 2)),
        ((products, 3),),
    )
    load_c.wait()
    load_f.wait()
    for t in range(len(turns) + max(LAGS)):
        for k in range(BLOCKS):
            if 0 <= t - LAGS[k] < len(turns):
                for step, *args in turns[t - LAGS[k]]:
                    step(k, *args)
            if t == 0 and k < 2:
                left_of_c(2 * k, 2 * k + 2)
    send_strips()
    for k in range(BLOCKS):
        send_parts(k)
    send_strip_sums()
    spread_grams()
    for k in range(BLOCKS):
        send_sums(k)
    swap_grams()
    solve(0)
    planes[7].wait_recv()
    solve(1)
    solve(2)
    update((0, 1, 2), True)
    for copy in sends:
        copy.wait_send()
    for store in stores:
        store.wait()


def shards(vectors, panels, factors, owners):
    any_space = pl.BlockSpec(memory_space=pl.ANY)
    dma = pltpu.SemaphoreType.DMA
    tall = (ROWS, WIDTH)
    square = (WIDTH, WIDTH)
    return pl.pallas_call(
        kernel,
        out_shape=jax.ShapeDtypeStruct(tall, F32),
        in_specs=[pl.BlockSpec(memory_space=pltpu.SMEM), any_space, any_space, any_space],
        out_specs=any_space,
        scratch_shapes=[
            pltpu.VMEM(tall, F32),
            pltpu.VMEM((BLOCKS, *square), F32),
            pltpu.VMEM((2 * WIDTH, ROWS), BF16),
            pltpu.VMEM((2 * WIDTH, ROWS), BF16),
            *[pltpu.VMEM(tall, F32)] * BLOCKS,
            pltpu.VMEM((BLOCKS, *tall), BF16),
            pltpu.VMEM((BLOCKS, *tall), BF16),
            *[pltpu.VMEM((8, p, WIDTH), F32) for p in PIECES],
            pltpu.VMEM((8, PIECES[0], WIDTH), F32),
            pltpu.VMEM((3, 8, PIECES[1], WIDTH), F32),
            *[pltpu.VMEM((BLOCKS, 2, LONG, p, WIDTH), F32) for p in PIECES],
            *[pltpu.VMEM((BLOCKS, 2, LONG, p, WIDTH), F32) for p in PIECES],
            pltpu.VMEM((BLOCKS, UNIT, WIDTH), F32),
            pltpu.VMEM((BLOCKS, UNIT, WIDTH), F32),
            pltpu.VMEM((BLOCKS, 8, SHARE, WIDTH), F32),
            pltpu.VMEM((BLOCKS, 8, SHARE, WIDTH), F32),
            pltpu.VMEM((BLOCKS, 7, SHARE, WIDTH), F32),
            pltpu.VMEM((HALF, WIDTH), F32),
            pltpu.VMEM((8, TILE, WIDTH), F32),
            pltpu.VMEM((7, TILE, WIDTH), F32),
            pltpu.VMEM((8, TILE, WIDTH), F32),
            pltpu.VMEM((2, 8, 6, TILE, WIDTH), F32),
            *[pltpu.VMEM((BLOCKS, *square), BF16)] * 4,
            dma((18,)),
            dma((4, 8)),
            dma((4, 8)),
            dma((2, BLOCKS, 2, LONG)),
            dma((2, BLOCKS, 2, LONG)),
            dma((BLOCKS,)),
            dma((BLOCKS,)),
            dma((BLOCKS, 2, 2, LONG)),
            dma((BLOCKS, 2, 2, LONG)),
            dma((BLOCKS, 8)),
            dma((BLOCKS, 8)),
            dma((BLOCKS, 3, 8)),
            dma((BLOCKS, 3, 8)),
            dma((BLOCKS, 2, 7)),
            dma((BLOCKS, 2, 7)),
            dma((2, 7)),
            dma((2, 7)),
            dma((7,)),
            dma((7,)),
            dma,
            dma,
        ],
        name="back_transform",
        compiler_params=pltpu.CompilerParams(
            collective_id=0, has_side_effects=True, vmem_limit_bytes=60 * 2**20
        ),
    )(owners, vectors, panels[0], factors)


def solution(mesh):
    placed = (P("row", "col"), P("col", "row", None), P(), P())
    return jax.shard_map(shards, mesh=mesh, in_specs=placed, out_specs=P("row", "col"), check_vma=False)
```

```python
import functools

import jax
import jax.numpy as jnp
from jax import lax
from jax.experimental import pallas as pl
from jax.experimental.pallas import tpu as pltpu
from jax.sharding import PartitionSpec as P

MESH = pl.DeviceIdType.MESH
F32, BF16 = jnp.float32, jnp.bfloat16
BLOCKS = 3
WIDTH = 256
HALF = WIDTH // 2
ROWS = 2048
GROUP = 256
CHUNK = 512
UNIT = 64
PIECES = (64, 32)
ORDER = (4, -3, 3, -2, 2, -1, 1, 0)
LONG, SHORT = 4, 3
HOPS = (LONG, SHORT)
SHARE = 32
STRIP = 16
PAIRS = ((0, 1), (0, 2), (1, 2))
TILE = 8
NN = (((1,), (0,)), ((), ()))
NT = (((1,), (1,)), ((), ()))


def halves(x):
    high = x.astype(BF16)
    return high, (x - high.astype(F32)).astype(BF16)


def dot3(a, b, dims=NN):
    def one(p, q):
        return lax.dot_general(p, q, dims, preferred_element_type=F32)

    return one(a[0], b[0]) + (one(a[0], b[1]) + one(a[1], b[0]))


def kernel(
    owners, c_ref, panel_ref, factors_ref, o_ref,
    c_v, f_v, left_hi, left_lo, v0, v1, v2, v_hi, v_lo,
    own_a, own_b, got_a, got_b, mine_a, mine_b, passed_a, passed_b, half_a, other_a,
    part, total, arrived, strip, strip_in, tile, tile_in, tile_sum, gram, yt_hi, yt_lo, y_hi, y_lo,
    local_sem, first_s, first_r, rs_s, rs_r, beside_s, beside_r, ag_s, ag_r, side_s, side_r, core_s, core_r, row_s, row_r,
    strip_s, strip_r, plane_s, plane_r, gram_s, gram_r,
):
    v = (v0, v1, v2)
    mine, passed = (mine_a, mine_b), (passed_a, passed_b)
    row, col = lax.axis_index("row"), lax.axis_index("col")
    yh, x = row // 4, row % 4
    yl, z, h = col // 16, (col // 2) % 8, col % 2
    sign = 1 - 2 * h

    def along(where):
        return lax.rem(z + 8 + where, 8)

    def at(dyl, dz, dh):
        return (row, (yl ^ dyl) * 16 + along(dz) * 2 + (h ^ dh))

    def unit_rows(u, half, where):
        return pl.ds(pl.multiple_of(along(where) * GROUP + half * (GROUP // 2) + u * UNIT, UNIT), UNIT)

    def small_rows(half, y, where):
        start = along(where) * GROUP + half * (GROUP // 2) + UNIT + y * PIECES[1]
        return pl.ds(pl.multiple_of(start, PIECES[1]), PIECES[1])

    def group_rows(where):
        return pl.ds(pl.multiple_of(along(where) * GROUP, GROUP), GROUP)

    def remote(src, dst, send, recv, device):
        return pltpu.make_async_remote_copy(
            src_ref=src, dst_ref=dst, send_sem=send, recv_sem=recv, device_id=device, device_id_type=MESH
        )

    sibling, partner, diagonal = at(0, 0, 1), at(1, 0, 0), at(1, 0, 1)
    ahead, behind = at(0, sign, 0), at(0, -sign, 0)
    peers = [((yh ^ (i // 4)) * 4 + (x + i % 4) % 4, col) for i in range(1, 8)]

    barrier = pltpu.get_barrier_semaphore()
    mates = [at(0, i, 0) for i in range(1, 8)]
    everyone = [sibling, partner, diagonal] + mates + peers
    for device in everyone:
        pl.semaphore_signal(barrier, inc=1, device_id=device, device_id_type=MESH)

    load_c = pltpu.make_async_copy(c_ref, c_v, local_sem.at[0])
    load_f = pltpu.make_async_copy(factors_ref, f_v, local_sem.at[1])
    loads = []
    for i, rel in enumerate(ORDER):
        where = sign * rel
        loads.append(
            (
                pltpu.make_async_copy(panel_ref.at[unit_rows(0, h, where)], own_a.at[i], local_sem.at[2 + i]),
                pltpu.make_async_copy(panel_ref.at[small_rows(h, yl, where)], own_b.at[i], local_sem.at[10 + i]),
            )
        )
        for load in loads[-1]:
            load.start()
    load_c.start()
    load_f.start()

    held = (col, col ^ 16, col ^ 17, col ^ 1)
    weight = [[jnp.where(owners[k] == c, 1.0, 0.0).astype(F32) for c in held] for k in range(BLOCKS)]

    pl.semaphore_wait(barrier, len(everyone))

    sends = []

    def go(copy):
        copy.start()
        sends.append(copy)
        return copy

    first = [[None] * 4 for _ in ORDER]

    def bring(n):
        for i, rel in enumerate(ORDER):
            same, turned = sign * rel, -sign * rel
            src, dst, device = (
                (panel_ref.at[unit_rows(0, 1 - h, turned)], got_a.at[i], sibling),
                (panel_ref.at[small_rows(h, 1 - yl, same)], got_b.at[0, i], partner),
                (panel_ref.at[small_rows(1 - h, 1 - yl, turned)], got_b.at[1, i], diagonal),
                (panel_ref.at[small_rows(1 - h, yl, turned)], got_b.at[2, i], sibling),
            )[n]
            first[i][n] = go(remote(src, dst, first_s.at[n, i], first_r.at[n, i], device))

    for n in range(4):
        bring(n)

    ready = set()

    def masked(u, k, i):
        if (u, i) not in ready:
            ready.add((u, i))
            loads[i][u].wait()
            for copy in first[i][1:] if u else first[i][:1]:
                copy.wait_recv()
        w = weight[k]
        if u == 0:
            return w[0] * own_a[i] + w[3] * got_a[i]
        return w[0] * own_b[i] + w[1] * got_b[0, i] + w[2] * got_b[1, i] + w[3] * got_b[2, i]

    ring = {}

    def sum_step(u, k, s):
        for way, device in ((0, ahead), (1, behind)):
            if s >= HOPS[way]:
                continue
            value = masked(u, k, ORDER.index((HOPS[way] - s) * (1 - 2 * way)))
            if s:
                ring[u, k, way, s - 1].wait_recv()
                value += passed[u][k, way, s - 1]
            mine[u][k, way, s] = value
            ring[u, k, way, s] = go(
                remote(
                    mine[u].at[k, way, s],
                    passed[u].at[k, way, s],
                    rs_s.at[u, k, way, s],
                    rs_r.at[u, k, way, s],
                    device,
                )
            )

    def summed(u, k):
        value = masked(u, k, 7)
        for way in range(2):
            ring[u, k, way, HOPS[way] - 1].wait_recv()
            value += passed[u][k, way, HOPS[way] - 1]
        return value

    def left_of_c(begin, end):
        @pl.loop(begin, end)
        def _(j):
            rows = pl.ds(pl.multiple_of(j * CHUNK, CHUNK), CHUNK)
            high, low = halves(c_v[rows, :].T)
            left_hi[0:WIDTH, rows] = high
            left_lo[0:WIDTH, rows] = low

    beside, spread, side, shared = {}, {}, {}, {}

    def where_of(slot):
        return 0 if slot == 7 else sign * (slot - LONG + 1) if slot >= LONG else -sign * (slot + 1)

    def send_on(copies, key, rows, sems, device):
        k = key[0]
        copies[key] = go(remote(v[k].at[rows], v[k].at[rows], sems[0].at[key], sems[1].at[key], device))

    def share(k, kind, slot):
        where = where_of(slot)
        rows = unit_rows(0, h, where) if kind == 0 else small_rows(h, yl if kind == 1 else 1 - yl, where)
        send_on(shared, (k, kind, slot), rows, (core_s, core_r), sibling)

    def pass_on(k, u, way, s):
        where = -sign * (1 - 2 * way) * s
        rows = small_rows(h, yl, where) if u else unit_rows(0, h, where)
        send_on(spread, (k, u, way, s), rows, (ag_s, ag_r), behind if way else ahead)

    def cross(k, slot):
        send_on(side, (k, slot), small_rows(h, yl, where_of(slot)), (side_s, side_r), partner)

    def offer(k):
        half_a[k] = summed(0, k)
        beside[k] = go(remote(half_a.at[k], other_a.at[k], beside_s.at[k], beside_r.at[k], partner))

    def start(u, k):
        if u:
            v[k][small_rows(h, yl, 0), :] = summed(1, k)
        else:
            beside[k].wait_recv()
            v[k][unit_rows(0, h, 0), :] = half_a[k] + other_a[k]
        for way in range(2):
            pass_on(k, u, way, 0)
        if u:
            cross(k, 7)
        share(k, u, 7)

    def gather(u, k, s):
        for way in range(2):
            if s >= HOPS[way]:
                continue
            spread[k, u, way, s].wait_recv()
            if s + 1 < HOPS[way]:
                pass_on(k, u, way, s + 1)
            slot = way * LONG + s
            if u:
                cross(k, slot)
            share(k, u, slot)

    def slots_of(s):
        return (7,) if s < 0 else (s, LONG + s) if s < SHORT else (s,)

    def crossed(k, s):
        for slot in slots_of(s):
            side[k, slot].wait_recv()
            share(k, 2, slot)

    def products(k, s):
        for kind in range(3):
            for slot in slots_of(s):
                shared[k, kind, slot].wait_recv()
        for way in (1, -1) if 0 <= s < SHORT else (1,):
            rows = group_rows(way * (s + 1))
            value = v[k][rows, :]
            high, low = halves(value)
            v_hi[k, rows, :] = high
            v_lo[k, rows, :] = low
            out = dot3((left_hi[:, rows], left_lo[:, rows]), (high, low)).reshape(8, SHARE, WIDTH)
            if s < 0:
                part[k] = out
            else:
                part[k] += out

    added, told, strips, planes = {}, {}, {}, {}

    def send_parts(k):
        for i, device in enumerate(peers):
            added[k, i] = go(
                remote(part.at[k, device[0]], arrived.at[k, i], row_s.at[k, 0, i], row_r.at[k, 0, i], device)
            )

    def send_sums(k):
        value = part[k, row]
        for i in range(7):
            added[k, i].wait_recv()
            value += arrived[k, i]
        total[k, row] = value
        for i, device in enumerate(peers):
            told[k, i] = go(remote(total.at[k, row], total.at[k, row], row_s.at[k, 1, i], row_r.at[k, 1, i], device))

    def send_strips():
        rows = group_rows(0)
        cols = pl.ds(pl.multiple_of(h * HALF, HALF), HALF)
        left = [halves(v[b][rows, cols].T) for b in range(BLOCKS - 1)]
        for n, (b, k) in enumerate(PAIRS):
            out = dot3(left[b], (v_hi[k, rows, :], v_lo[k, rows, :]))
            strip[:, STRIP * n : STRIP * (n + 1), :] = out.reshape(8, STRIP, WIDTH)
        for i, device in enumerate(peers):
            strips[0, i] = go(remote(strip.at[device[0]], strip_in.at[i], strip_s.at[0, i], strip_r.at[0, i], device))

    def send_tiles():
        value = strip[row]
        for i in range(7):
            strips[0, i].wait_recv()
            value += strip_in[i]
        tile[0:6] = value.reshape(6, TILE, WIDTH)
        tile[6:8] = jnp.zeros((2, TILE, WIDTH), F32)
        for i, device in enumerate(mates):
            planes[0, i] = go(
                remote(tile.at[along(i + 1)], tile_in.at[i], plane_s.at[0, i], plane_r.at[0, i], device)
            )

    def send_tile_sums():
        value = tile[z]
        for i in range(7):
            planes[0, i].wait_recv()
            value += tile_in[i]
        tile_sum[z] = value
        for i, device in enumerate(mates):
            planes[1, i] = go(
                remote(tile_sum.at[z], tile_sum.at[z], plane_s.at[1, i], plane_r.at[1, i], device)
            )

    def spread_grams():
        for i in range(7):
            planes[1, i].wait_recv()
        gram[h, row] = tile_sum[0:6]
        for i, device in enumerate(peers):
            strips[1, i] = go(
                remote(gram.at[h, row], gram.at[h, row], strip_s.at[1, i], strip_r.at[1, i], device)
            )

    def swap_grams():
        for i in range(7):
            strips[1, i].wait_recv()
        planes[2] = go(remote(gram.at[h], gram.at[h], gram_s, gram_r, sibling))

    def solve(k):
        for i in range(7):
            told[k, i].wait_recv()
        value = total[k].reshape(WIDTH, WIDTH)
        for b in range(k):
            n = PAIRS.index((b, k))
            for half in range(2):
                value -= dot3(
                    (yt_hi[b, :, half * HALF : (half + 1) * HALF], yt_lo[b, :, half * HALF : (half + 1) * HALF]),
                    halves(gram[half, :, 2 * n : 2 * n + 2].reshape(HALF, WIDTH)),
                )
        value, factor = halves(value), halves(f_v[k])
        high, low = halves(dot3(factor, value, NT))
        y_hi[k] = high
        y_lo[k] = low
        if k + 1 < BLOCKS:
            high, low = halves(dot3(value, factor, NT))
            yt_hi[k] = high
            yt_lo[k] = low

    stores = []

    def update(blocks, last):
        for j in range(ROWS // CHUNK):
            rows = pl.ds(j * CHUNK, CHUNK)
            value = c_v[rows, :]
            for k in blocks:
                value -= dot3((v_hi[k, rows, :], v_lo[k, rows, :]), (y_hi[k], y_lo[k]))
            c_v[rows, :] = value
            if last:
                stores.append(pltpu.make_async_copy(c_v.at[rows], o_ref.at[rows], local_sem.at[2 + j]))
                stores[-1].start()

    def each(step, *args):
        for k in range(BLOCKS):
            step(*args[:1], k, *args[1:])

    A, B = functools.partial(sum_step, 0), functools.partial(sum_step, 1)
    gather_a, gather_b = functools.partial(gather, 0), functools.partial(gather, 1)
    turns = (
        ((A, 0),),
        ((A, 1),),
        ((A, 2),),
        ((A, 3), (B, 0)),
        ((offer,), (B, 1)),
        ((functools.partial(start, 0),), (B, 2)),
        ((gather_a, 0), (B, 3)),
        ((gather_a, 1), (functools.partial(start, 1),)),
        ((gather_a, 2), (gather_b, 0), (crossed, -1)),
        ((gather_a, 3), (gather_b, 1), (products, -1)),
        ((gather_b, 2), (crossed, 0)),
        ((gather_b, 3), (crossed, 1), (products, 0)),
        ((crossed, 2), (products, 1)),
        ((crossed, 3), (products, 2)),
        ((products, 3), (send_parts,)),
    )
    load_c.wait()
    load_f.wait()
    aside = {9: send_strips, 13: send_tiles, 14: send_tile_sums}
    for t, turn in enumerate(turns):
        for k in range(BLOCKS):
            for step, *args in turn:
                step(k, *args)
            if t == 0 and k < 2:
                left_of_c(2 * k, 2 * k + 2)
        if t in aside:
            aside[t]()
    spread_grams()
    for k in range(BLOCKS):
        send_sums(k)
    swap_grams()
    solve(0)
    planes[2].wait_recv()
    solve(1)
    solve(2)
    update((0, 1, 2), True)
    for copy in sends:
        copy.wait_send()
    for store in stores:
        store.wait()


def shards(vectors, panels, factors, owners):
    any_space = pl.BlockSpec(memory_space=pl.ANY)
    dma = pltpu.SemaphoreType.DMA
    tall = (ROWS, WIDTH)
    square = (WIDTH, WIDTH)
    return pl.pallas_call(
        kernel,
        out_shape=jax.ShapeDtypeStruct(tall, F32),
        in_specs=[pl.BlockSpec(memory_space=pltpu.SMEM), any_space, any_space, any_space],
        out_specs=any_space,
        scratch_shapes=[
            pltpu.VMEM(tall, F32),
            pltpu.VMEM((BLOCKS, *square), F32),
            pltpu.VMEM((WIDTH, ROWS), BF16),
            pltpu.VMEM((WIDTH, ROWS), BF16),
            *[pltpu.VMEM(tall, F32)] * BLOCKS,
            pltpu.VMEM((BLOCKS, *tall), BF16),
            pltpu.VMEM((BLOCKS, *tall), BF16),
            *[pltpu.VMEM((8, p, WIDTH), F32) for p in PIECES],
            pltpu.VMEM((8, PIECES[0], WIDTH), F32),
            pltpu.VMEM((3, 8, PIECES[1], WIDTH), F32),
            *[pltpu.VMEM((BLOCKS, 2, LONG, p, WIDTH), F32) for p in PIECES],
            *[pltpu.VMEM((BLOCKS, 2, LONG, p, WIDTH), F32) for p in PIECES],
            pltpu.VMEM((BLOCKS, UNIT, WIDTH), F32),
            pltpu.VMEM((BLOCKS, UNIT, WIDTH), F32),
            pltpu.VMEM((BLOCKS, 8, SHARE, WIDTH), F32),
            pltpu.VMEM((BLOCKS, 8, SHARE, WIDTH), F32),
            pltpu.VMEM((BLOCKS, 7, SHARE, WIDTH), F32),
            pltpu.VMEM((8, 3 * STRIP, WIDTH), F32),
            pltpu.VMEM((7, 3 * STRIP, WIDTH), F32),
            pltpu.VMEM((8, TILE, WIDTH), F32),
            pltpu.VMEM((7, TILE, WIDTH), F32),
            pltpu.VMEM((8, TILE, WIDTH), F32),
            pltpu.VMEM((2, 8, 6, TILE, WIDTH), F32),
            *[pltpu.VMEM((BLOCKS, *square), BF16)] * 4,
            dma((18,)),
            dma((4, 8)),
            dma((4, 8)),
            dma((2, BLOCKS, 2, LONG)),
            dma((2, BLOCKS, 2, LONG)),
            dma((BLOCKS,)),
            dma((BLOCKS,)),
            dma((BLOCKS, 2, 2, LONG)),
            dma((BLOCKS, 2, 2, LONG)),
            dma((BLOCKS, 8)),
            dma((BLOCKS, 8)),
            dma((BLOCKS, 3, 8)),
            dma((BLOCKS, 3, 8)),
            dma((BLOCKS, 2, 7)),
            dma((BLOCKS, 2, 7)),
            dma((2, 7)),
            dma((2, 7)),
            dma((2, 7)),
            dma((2, 7)),
            dma,
            dma,
        ],
        name="back_transform",
        compiler_params=pltpu.CompilerParams(
            collective_id=0, has_side_effects=True, vmem_limit_bytes=60 * 2**20
        ),
    )(owners, vectors, panels[0], factors)


def solution(mesh):
    placed = (P("row", "col"), P("col", "row", None), P(), P())
    return jax.shard_map(shards, mesh=mesh, in_specs=placed, out_specs=P("row", "col"), check_vma=False)
```

```python
import functools

import jax
import jax.numpy as jnp
from jax import lax
from jax.experimental import pallas as pl
from jax.experimental.pallas import tpu as pltpu
from jax.sharding import PartitionSpec as P

MESH = pl.DeviceIdType.MESH
F32, BF16 = jnp.float32, jnp.bfloat16
BLOCKS = 3
WIDTH = 256
HALF = WIDTH // 2
ROWS = 2048
GROUP = 256
CHUNK = 512
UNIT = 64
PIECES = (64, 32)
ORDER = (4, -3, 3, -2, 2, -1, 1, 0)
LONG, SHORT = 4, 3
HOPS = (LONG, SHORT)
SHARE = 32
STRIP = 16
PAIRS = ((0, 1), (0, 2), (1, 2))
TILE = 8
NN = (((1,), (0,)), ((), ()))
NT = (((1,), (1,)), ((), ()))


def halves(x):
    high = x.astype(BF16)
    return high, (x - high.astype(F32)).astype(BF16)


def dot3(a, b, dims=NN):
    def one(p, q):
        return lax.dot_general(p, q, dims, preferred_element_type=F32)

    return one(a[0], b[0]) + (one(a[0], b[1]) + one(a[1], b[0]))


def kernel(
    owners, c_ref, panel_ref, factors_ref, o_ref,
    c_v, f_v, left_hi, left_lo, v0, v1, v2, v_hi, v_lo,
    own_a, own_b, got_a, got_b, mine_a, mine_b, passed_a, passed_b, half_a, other_a,
    part, total, arrived, strip, strip_in, tile, tile_in, tile_sum, gram, yt_hi, yt_lo, y_hi, y_lo,
    local_sem, first_s, first_r, rs_s, rs_r, beside_s, beside_r, ag_s, ag_r, side_s, side_r, core_s, core_r, row_s, row_r,
    strip_s, strip_r, plane_s, plane_r, gram_s, gram_r,
):
    v = (v0, v1, v2)
    mine, passed = (mine_a, mine_b), (passed_a, passed_b)
    row, col = lax.axis_index("row"), lax.axis_index("col")
    yh, x = row // 4, row % 4
    yl, z, h = col // 16, (col // 2) % 8, col % 2
    sign = 1 - 2 * h

    def along(where):
        return lax.rem(z + 8 + where, 8)

    def at(dyl, dz, dh):
        return (row, (yl ^ dyl) * 16 + along(dz) * 2 + (h ^ dh))

    def unit_rows(u, half, where):
        return pl.ds(pl.multiple_of(along(where) * GROUP + half * (GROUP // 2) + u * UNIT, UNIT), UNIT)

    def small_rows(half, y, where):
        start = along(where) * GROUP + half * (GROUP // 2) + UNIT + y * PIECES[1]
        return pl.ds(pl.multiple_of(start, PIECES[1]), PIECES[1])

    def group_rows(where):
        return pl.ds(pl.multiple_of(along(where) * GROUP, GROUP), GROUP)

    def remote(src, dst, send, recv, device):
        return pltpu.make_async_remote_copy(
            src_ref=src, dst_ref=dst, send_sem=send, recv_sem=recv, device_id=device, device_id_type=MESH
        )

    sibling, partner, diagonal = at(0, 0, 1), at(1, 0, 0), at(1, 0, 1)
    ahead, behind = at(0, sign, 0), at(0, -sign, 0)
    peers = [((yh ^ (i // 4)) * 4 + (x + i % 4) % 4, col) for i in range(1, 8)]

    barrier = pltpu.get_barrier_semaphore()
    mates = [at(0, i, 0) for i in range(1, 8)]
    everyone = [sibling, partner, diagonal] + mates + peers
    for device in everyone:
        pl.semaphore_signal(barrier, inc=1, device_id=device, device_id_type=MESH)

    load_c = pltpu.make_async_copy(c_ref, c_v, local_sem.at[0])
    load_f = pltpu.make_async_copy(factors_ref, f_v, local_sem.at[1])
    loads = []
    for i, rel in enumerate(ORDER):
        where = sign * rel
        loads.append(
            (
                pltpu.make_async_copy(panel_ref.at[unit_rows(0, h, where)], own_a.at[i], local_sem.at[2 + i]),
                pltpu.make_async_copy(panel_ref.at[small_rows(h, yl, where)], own_b.at[i], local_sem.at[10 + i]),
            )
        )
        for load in loads[-1]:
            load.start()
    load_c.start()
    load_f.start()

    held = (col, col ^ 16, col ^ 17, col ^ 1)
    weight = [[jnp.where(owners[k] == c, 1.0, 0.0).astype(F32) for c in held] for k in range(BLOCKS)]

    pl.semaphore_wait(barrier, len(everyone))

    sends = []

    def go(copy):
        copy.start()
        sends.append(copy)
        return copy

    first = [[None] * 4 for _ in ORDER]

    def bring(n):
        for i, rel in enumerate(ORDER):
            same, turned = sign * rel, -sign * rel
            src, dst, device = (
                (panel_ref.at[unit_rows(0, 1 - h, turned)], got_a.at[i], sibling),
                (panel_ref.at[small_rows(h, 1 - yl, same)], got_b.at[0, i], partner),
                (panel_ref.at[small_rows(1 - h, 1 - yl, turned)], got_b.at[1, i], diagonal),
                (panel_ref.at[small_rows(1 - h, yl, turned)], got_b.at[2, i], sibling),
            )[n]
            first[i][n] = go(remote(src, dst, first_s.at[n, i], first_r.at[n, i], device))

    for n in range(4):
        bring(n)

    ready = set()

    def masked(u, k, i):
        if (u, i) not in ready:
            ready.add((u, i))
            loads[i][u].wait()
            for copy in first[i][1:] if u else first[i][:1]:
                copy.wait_recv()
        w = weight[k]
        if u == 0:
            return w[0] * own_a[i] + w[3] * got_a[i]
        return w[0] * own_b[i] + w[1] * got_b[0, i] + w[2] * got_b[1, i] + w[3] * got_b[2, i]

    ring = {}

    def sum_step(u, k, s):
        for way, device in ((0, ahead), (1, behind)):
            if s >= HOPS[way]:
                continue
            value = masked(u, k, ORDER.index((HOPS[way] - s) * (1 - 2 * way)))
            if s:
                ring[u, k, way, s - 1].wait_recv()
                value += passed[u][k, way, s - 1]
            mine[u][k, way, s] = value
            ring[u, k, way, s] = go(
                remote(
                    mine[u].at[k, way, s],
                    passed[u].at[k, way, s],
                    rs_s.at[u, k, way, s],
                    rs_r.at[u, k, way, s],
                    device,
                )
            )

    def summed(u, k):
        value = masked(u, k, 7)
        for way in range(2):
            ring[u, k, way, HOPS[way] - 1].wait_recv()
            value += passed[u][k, way, HOPS[way] - 1]
        return value

    def left_of_c(begin, end):
        @pl.loop(begin, end)
        def _(j):
            rows = pl.ds(pl.multiple_of(j * CHUNK, CHUNK), CHUNK)
            high, low = halves(c_v[rows, :].T)
            left_hi[0:WIDTH, rows] = high
            left_lo[0:WIDTH, rows] = low

    beside, spread, side, shared = {}, {}, {}, {}

    def where_of(slot):
        return 0 if slot == 7 else sign * (slot - LONG + 1) if slot >= LONG else -sign * (slot + 1)

    def send_on(copies, key, rows, sems, device):
        k = key[0]
        copies[key] = go(remote(v[k].at[rows], v[k].at[rows], sems[0].at[key], sems[1].at[key], device))

    def share(k, kind, slot):
        where = where_of(slot)
        rows = unit_rows(0, h, where) if kind == 0 else small_rows(h, yl if kind == 1 else 1 - yl, where)
        send_on(shared, (k, kind, slot), rows, (core_s, core_r), sibling)

    def pass_on(k, u, way, s):
        where = -sign * (1 - 2 * way) * s
        rows = small_rows(h, yl, where) if u else unit_rows(0, h, where)
        send_on(spread, (k, u, way, s), rows, (ag_s, ag_r), behind if way else ahead)

    def cross(k, slot):
        send_on(side, (k, slot), small_rows(h, yl, where_of(slot)), (side_s, side_r), partner)

    def offer(k):
        half_a[k] = summed(0, k)
        beside[k] = go(remote(half_a.at[k], other_a.at[k], beside_s.at[k], beside_r.at[k], partner))

    def start(u, k):
        if u:
            v[k][small_rows(h, yl, 0), :] = summed(1, k)
        else:
            beside[k].wait_recv()
            v[k][unit_rows(0, h, 0), :] = half_a[k] + other_a[k]
        for way in range(2):
            pass_on(k, u, way, 0)
        if u:
            cross(k, 7)
        share(k, u, 7)

    def gather(u, k, s):
        for way in range(2):
            if s >= HOPS[way]:
                continue
            spread[k, u, way, s].wait_recv()
            if s + 1 < HOPS[way]:
                pass_on(k, u, way, s + 1)
            slot = way * LONG + s
            if u:
                cross(k, slot)
            share(k, u, slot)

    def slots_of(s):
        return (7,) if s < 0 else (s, LONG + s) if s < SHORT else (s,)

    def crossed(k, s):
        for slot in slots_of(s):
            side[k, slot].wait_recv()
            share(k, 2, slot)

    def products(k, s):
        for kind in range(3):
            for slot in slots_of(s):
                shared[k, kind, slot].wait_recv()
        for way in (1, -1) if 0 <= s < SHORT else (1,):
            rows = group_rows(way * (s + 1))
            value = v[k][rows, :]
            high, low = halves(value)
            v_hi[k, rows, :] = high
            v_lo[k, rows, :] = low
            out = dot3((left_hi[:, rows], left_lo[:, rows]), (high, low)).reshape(8, SHARE, WIDTH)
            if s < 0:
                part[k] = out
            else:
                part[k] += out

    added, told, strips, planes = {}, {}, {}, {}

    def send_parts(k):
        for i, device in enumerate(peers):
            added[k, i] = go(
                remote(part.at[k, device[0]], arrived.at[k, i], row_s.at[k, 0, i], row_r.at[k, 0, i], device)
            )

    def send_sums(k):
        value = part[k, row]
        for i in range(7):
            added[k, i].wait_recv()
            value += arrived[k, i]
        total[k, row] = value
        for i, device in enumerate(peers):
            told[k, i] = go(remote(total.at[k, row], total.at[k, row], row_s.at[k, 1, i], row_r.at[k, 1, i], device))

    def send_strips():
        rows = group_rows(0)
        cols = pl.ds(pl.multiple_of(h * HALF, HALF), HALF)
        left = [halves(v[b][rows, cols].T) for b in range(BLOCKS - 1)]
        for n, (b, k) in enumerate(PAIRS):
            out = dot3(left[b], (v_hi[k, rows, :], v_lo[k, rows, :]))
            strip[:, STRIP * n : STRIP * (n + 1), :] = out.reshape(8, STRIP, WIDTH)
        for i, device in enumerate(peers):
            strips[0, i] = go(remote(strip.at[device[0]], strip_in.at[i], strip_s.at[0, i], strip_r.at[0, i], device))

    def send_tiles():
        value = strip[row]
        for i in range(7):
            strips[0, i].wait_recv()
            value += strip_in[i]
        tile[0:6] = value.reshape(6, TILE, WIDTH)
        tile[6:8] = jnp.zeros((2, TILE, WIDTH), F32)
        for i, device in enumerate(mates):
            planes[0, i] = go(
                remote(tile.at[along(i + 1)], tile_in.at[i], plane_s.at[0, i], plane_r.at[0, i], device)
            )

    def send_tile_sums():
        value = tile[z]
        for i in range(7):
            planes[0, i].wait_recv()
            value += tile_in[i]
        tile_sum[z] = value
        for i, device in enumerate(mates):
            planes[1, i] = go(
                remote(tile_sum.at[z], tile_sum.at[z], plane_s.at[1, i], plane_r.at[1, i], device)
            )

    def spread_grams():
        for i in range(7):
            planes[1, i].wait_recv()
        gram[h, row] = tile_sum[0:6]
        for i, device in enumerate(peers):
            strips[1, i] = go(
                remote(gram.at[h, row], gram.at[h, row], strip_s.at[1, i], strip_r.at[1, i], device)
            )

    def swap_grams():
        for i in range(7):
            strips[1, i].wait_recv()
        planes[2] = go(remote(gram.at[h], gram.at[h], gram_s, gram_r, sibling))

    def solve(k):
        for i in range(7):
            told[k, i].wait_recv()
        value = total[k].reshape(WIDTH, WIDTH)
        for b in range(k):
            n = PAIRS.index((b, k))
            for half in range(2):
                value -= dot3(
                    (yt_hi[b, :, half * HALF : (half + 1) * HALF], yt_lo[b, :, half * HALF : (half + 1) * HALF]),
                    halves(gram[half, :, 2 * n : 2 * n + 2].reshape(HALF, WIDTH)),
                )
        value, factor = halves(value), halves(f_v[k])
        high, low = halves(dot3(factor, value, NT))
        y_hi[k] = high
        y_lo[k] = low
        if k + 1 < BLOCKS:
            high, low = halves(dot3(value, factor, NT))
            yt_hi[k] = high
            yt_lo[k] = low

    stores = []

    def update(blocks, last):
        for j in range(ROWS // CHUNK):
            rows = pl.ds(j * CHUNK, CHUNK)
            value = c_v[rows, :]
            for k in blocks:
                value -= dot3((v_hi[k, rows, :], v_lo[k, rows, :]), (y_hi[k], y_lo[k]))
            c_v[rows, :] = value
            if last:
                stores.append(pltpu.make_async_copy(c_v.at[rows], o_ref.at[rows], local_sem.at[2 + j]))
                stores[-1].start()

    def each(step, *args):
        for k in range(BLOCKS):
            step(*args[:1], k, *args[1:])

    A, B = functools.partial(sum_step, 0), functools.partial(sum_step, 1)
    gather_a, gather_b = functools.partial(gather, 0), functools.partial(gather, 1)
    turns = (
        ((A, 0),),
        ((A, 1),),
        ((A, 2),),
        ((A, 3), (B, 0)),
        ((offer,), (B, 1)),
        ((functools.partial(start, 0),), (B, 2)),
        ((gather_a, 0), (B, 3)),
        ((gather_a, 1), (functools.partial(start, 1),)),
        ((gather_a, 2), (gather_b, 0), (crossed, -1)),
        ((gather_a, 3), (gather_b, 1), (products, -1)),
        ((gather_b, 2), (crossed, 0)),
        ((gather_b, 3), (crossed, 1), (products, 0)),
        ((crossed, 2), (products, 1)),
        ((crossed, 3), (products, 2)),
        ((products, 3), (send_parts,)),
    )
    load_c.wait()
    load_f.wait()
    aside = {9: send_strips, 13: send_tiles, 14: send_tile_sums}
    for t, turn in enumerate(turns):
        for k in range(BLOCKS):
            for step, *args in turn:
                step(k, *args)
            if t == 0 and k < 2:
                left_of_c(2 * k, 2 * k + 2)
        if t in aside:
            aside[t]()
    spread_grams()
    for k in range(BLOCKS):
        send_sums(k)
    swap_grams()
    solve(0)
    planes[2].wait_recv()
    solve(1)
    update((0, 1), False)
    solve(2)
    update((2,), True)
    for copy in sends:
        copy.wait_send()
    for store in stores:
        store.wait()


def shards(vectors, panels, factors, owners):
    any_space = pl.BlockSpec(memory_space=pl.ANY)
    dma = pltpu.SemaphoreType.DMA
    tall = (ROWS, WIDTH)
    square = (WIDTH, WIDTH)
    return pl.pallas_call(
        kernel,
        out_shape=jax.ShapeDtypeStruct(tall, F32),
        in_specs=[pl.BlockSpec(memory_space=pltpu.SMEM), any_space, any_space, any_space],
        out_specs=any_space,
        scratch_shapes=[
            pltpu.VMEM(tall, F32),
            pltpu.VMEM((BLOCKS, *square), F32),
            pltpu.VMEM((WIDTH, ROWS), BF16),
            pltpu.VMEM((WIDTH, ROWS), BF16),
            *[pltpu.VMEM(tall, F32)] * BLOCKS,
            pltpu.VMEM((BLOCKS, *tall), BF16),
            pltpu.VMEM((BLOCKS, *tall), BF16),
            *[pltpu.VMEM((8, p, WIDTH), F32) for p in PIECES],
            pltpu.VMEM((8, PIECES[0], WIDTH), F32),
            pltpu.VMEM((3, 8, PIECES[1], WIDTH), F32),
            *[pltpu.VMEM((BLOCKS, 2, LONG, p, WIDTH), F32) for p in PIECES],
            *[pltpu.VMEM((BLOCKS, 2, LONG, p, WIDTH), F32) for p in PIECES],
            pltpu.VMEM((BLOCKS, UNIT, WIDTH), F32),
            pltpu.VMEM((BLOCKS, UNIT, WIDTH), F32),
            pltpu.VMEM((BLOCKS, 8, SHARE, WIDTH), F32),
            pltpu.VMEM((BLOCKS, 8, SHARE, WIDTH), F32),
            pltpu.VMEM((BLOCKS, 7, SHARE, WIDTH), F32),
            pltpu.VMEM((8, 3 * STRIP, WIDTH), F32),
            pltpu.VMEM((7, 3 * STRIP, WIDTH), F32),
            pltpu.VMEM((8, TILE, WIDTH), F32),
            pltpu.VMEM((7, TILE, WIDTH), F32),
            pltpu.VMEM((8, TILE, WIDTH), F32),
            pltpu.VMEM((2, 8, 6, TILE, WIDTH), F32),
            *[pltpu.VMEM((BLOCKS, *square), BF16)] * 4,
            dma((18,)),
            dma((4, 8)),
            dma((4, 8)),
            dma((2, BLOCKS, 2, LONG)),
            dma((2, BLOCKS, 2, LONG)),
            dma((BLOCKS,)),
            dma((BLOCKS,)),
            dma((BLOCKS, 2, 2, LONG)),
            dma((BLOCKS, 2, 2, LONG)),
            dma((BLOCKS, 8)),
            dma((BLOCKS, 8)),
            dma((BLOCKS, 3, 8)),
            dma((BLOCKS, 3, 8)),
            dma((BLOCKS, 2, 7)),
            dma((BLOCKS, 2, 7)),
            dma((2, 7)),
            dma((2, 7)),
            dma((2, 7)),
            dma((2, 7)),
            dma,
            dma,
        ],
        name="back_transform",
        compiler_params=pltpu.CompilerParams(
            collective_id=0, has_side_effects=True, vmem_limit_bytes=60 * 2**20
        ),
    )(owners, vectors, panels[0], factors)


def solution(mesh):
    placed = (P("row", "col"), P("col", "row", None), P(), P())
    return jax.shard_map(shards, mesh=mesh, in_specs=placed, out_specs=P("row", "col"), check_vma=False)
```
